256 devices in a mesh: leaf: 32 (over x, z), rows: 8 (over y, core).
Axes of the slice: x: 4, y: 4, z: 8, core: 2. Of those that a mesh axis runs over, the one named last changes fastest.
Arguments:
- leaf_basis: float32 [8192, 64, 256], P(('leaf', 'rows')), may hold values from -0.375 to 0.375
- leaf_transfer: float32 [8192, 64, 64], P(('leaf', 'rows'))
- device_transfer: float32 [256, 64, 64], P(('leaf', 'rows'))
- upper_transfer: float32 [254, 64, 64], replicated
- couplings: float32 [8192, 64, 64], P(('leaf', 'rows')), may hold values from -0.1875 to 0.1875
- couple_offset: int32 [8192], P(('leaf', 'rows')), may hold values from 8 to 248, as said below
Outputs:
- leaf_orth: float32 [8192, 64, 256], P(('leaf', 'rows'))
- leaf_bridge: float32 [8192, 64, 64], P(('leaf', 'rows'))
- new_transfers: float32 [256, 8, 64, 64], P(('leaf', 'rows'))
- coupled: float32 [8192, 64, 64], P(('leaf', 'rows'))
The draws below stay inside these ranges and needn't reach their ends.
Inputs may be any that keep to these rules, and one draw needn't show every extreme that they name: couple_offset[b] is 8 times a number of 1 to 31, so block b couples device cluster b // 32 with a cluster of another branch at the same position within its branch; among the 32 blocks of one device cluster, at most 2 name the same column cluster, and on every device some column cluster is named exactly 2 times.
All inputs are finite; a program needn't handle non-finite values.
Results may differ from the reference program's by a relative error of at most 0.0001.
Values sent between devices are 32-bit elements; how exact they have to be, the bound alone decides.
A program may use at most 128 MiB of HBM per device.

```python
import jax
import jax.numpy as jnp
from jax import lax

LEAF = 256
RANK = 64
LEAF_DEV = 32
BLK_DEV = 32
LEAVES = 8192
BLOCKS = 8192
N_LEAF = 32
N_ROWS = 8


def near_identity(noise):
    eye = (lax.broadcasted_iota(jnp.int32, (RANK, RANK), 0) == lax.broadcasted_iota(jnp.int32, (RANK, RANK), 1)).astype(jnp.float32)
    return eye[None] + 0.3 / RANK ** 0.5 * noise


def draw_leaf_transfer(key, part):
    key = jax.random.fold_in(key, 11)
    shape = (LEAF_DEV * N_LEAF * N_ROWS, RANK, RANK)
    noise = jax.random.normal(key, shape, jnp.float32)
    return near_identity(noise)


def draw_device_transfer(key, part):
    key = jax.random.fold_in(key, 23)
    shape = (N_LEAF * N_ROWS, RANK, RANK)
    noise = jax.random.normal(key, shape, jnp.float32)
    return near_identity(noise)


def draw_upper_transfer(key, part):
    key = jax.random.fold_in(key, 37)
    shape = (N_LEAF * N_ROWS - 2, RANK, RANK)
    noise = jax.random.normal(key, shape, jnp.float32)
    return near_identity(noise)


def draw_couple_offset(key, part):
    key = jax.random.fold_in(key, 41)
    clusters = N_LEAF * N_ROWS
    others = N_LEAF - 1
    scores = jax.random.randint(key, (clusters, others), 0, 1 << 20)
    scores = scores * others + lax.broadcasted_iota(jnp.int32, (clusters, others), 1)
    order = jnp.argsort(scores, axis=1).astype(jnp.int32)
    slots = lax.broadcasted_iota(jnp.int32, (clusters, BLK_DEV), 1)
    picks = jnp.maximum(slots - 1, 0) % others
    chosen = jnp.take_along_axis(order, picks, axis=1) + 1
    return (N_ROWS * chosen).reshape(clusters * BLK_DEV).astype(jnp.int32)


def steps_of(stream_key, extent, shards, low, top_value):
    loudness = 1.0
    for dim, blocks in shards:
        steps = jax.random.uniform(jax.random.fold_in(jax.random.fold_in(stream_key, 6), dim), (blocks,), jnp.float32, low / len(shards), top_value / len(shards))
        loudness = loudness * jnp.repeat(jnp.exp(steps), extent[dim] // blocks).reshape((-1,) + (1,) * (len(extent) - 1 - dim))
    return loudness


def normal_values(rng, extent, spread, reach, cuts=(), kind=jnp.bfloat16):
    result = jax.random.normal(rng, extent, jnp.float32) * spread
    if len(cuts) > 0:
        result = steps_of(rng, extent, cuts, -0.22, 0.18) * result
    return jnp.clip(result, min=-reach, max=reach).astype(kind)


def setup_inputs(seed: int = 0) -> dict:
    seeds = jax.random.split(jax.random.key(seed), 7)
    leaf_basis = normal_values(seeds[0], (LEAVES, RANK, LEAF), 0.0625, 0.375, ((0, 256),), jnp.float32)
    leaf_transfer = draw_leaf_transfer(jax.random.fold_in(seeds[6], 71), 0)
    device_transfer = draw_device_transfer(jax.random.fold_in(seeds[6], 71), 0)
    upper_transfer = draw_upper_transfer(jax.random.fold_in(seeds[6], 71), 0)
    couplings = normal_values(seeds[4], (BLOCKS, RANK, RANK), (1.0 / LEAF_DEV), 0.1875, ((0, 256),), jnp.float32)
    couple_offset = draw_couple_offset(jax.random.fold_in(seeds[6], 71), 0)
    return {"leaf_basis": leaf_basis, "leaf_transfer": leaf_transfer, "device_transfer": device_transfer, "upper_transfer": upper_transfer, "couplings": couplings, "couple_offset": couple_offset}


HIGH = lax.Precision.HIGHEST

def lower_solve(low, right):
    return lax.linalg.triangular_solve(low, right, left_side=True, lower=True)

def lift(grams, trans):
    inner = jnp.einsum('nkl,nlj->nkj', grams, trans, precision=HIGH)
    return jnp.einsum('nki,nkj->nij', trans, inner, precision=HIGH)

def reference(leaf_basis, leaf_transfer, device_transfer, upper_transfer, couplings, couple_offset):
    clusters = N_LEAF * N_ROWS
    levels = clusters.bit_length() - 1
    leaf_gram = jnp.einsum('nrk,nsk->nrs', leaf_basis, leaf_basis, precision=HIGH)
    leaf_low = jnp.linalg.cholesky(leaf_gram)
    leaf_orth = lower_solve(leaf_low, leaf_basis)
    moved = lift(leaf_gram, leaf_transfer)
    device_gram = jnp.sum(moved.reshape(clusters, LEAF_DEV, RANK, RANK), axis=1)
    grams = [device_gram]
    transfers = [device_transfer]
    lifted = lift(device_gram, device_transfer)
    for level in range(levels - 1, -1, -1):
        gram = lifted[0::2] + lifted[1::2]
        grams.append(gram)
        if level > 0:
            trans = upper_transfer[2 ** level - 2:2 ** (level + 1) - 2]
            transfers.append(trans)
            lifted = lift(gram, trans)
    lows = [jnp.linalg.cholesky(gram) for gram in grams]
    columns = []
    for step in range(levels):
        parent = jnp.repeat(lows[step + 1], 2, axis=0)
        right = jnp.einsum('nki,nkj->nij', transfers[step], lows[step], precision=HIGH)
        fresh = jnp.swapaxes(lower_solve(parent, right), 1, 2)
        columns.append(jnp.repeat(fresh, 2 ** step, axis=0))
    new_transfers = jnp.stack(columns, axis=1)
    device_low = jnp.repeat(lows[0], LEAF_DEV, axis=0)
    right = jnp.einsum('nki,nkj->nij', leaf_transfer, leaf_low, precision=HIGH)
    leaf_bridge = jnp.swapaxes(lower_solve(device_low, right), 1, 2)
    owners = (jnp.arange(BLK_DEV * clusters, dtype=jnp.int32) // BLK_DEV).astype(jnp.int32)
    targets = ((owners + couple_offset) % clusters).astype(jnp.int32)
    row_low = jnp.take(lows[0], owners, axis=0)
    col_low = jnp.take(lows[0], targets, axis=0)
    inner = jnp.einsum('nkl,nlj->nkj', couplings, col_low, precision=HIGH)
    coupled = jnp.einsum('nki,nkj->nij', row_low, inner, precision=HIGH)
    return (leaf_orth, leaf_bridge, new_transfers, coupled)
```

```python
import functools

import jax
import jax.numpy as jnp
from jax import lax
from jax.experimental import pallas as pl
from jax.experimental.pallas import tpu as pltpu
from jax.sharding import PartitionSpec as P

HIGH = lax.Precision.HIGHEST
RANK = 64
Z_BITS = 3


def mm(a, b, dims="nn"):
    contract = ((1 if dims[0] == "n" else 0,), (0 if dims[1] == "n" else 1,))
    return lax.dot_general(
        a, b, (contract, ((), ())), precision=HIGH, preferred_element_type=jnp.float32
    )


def lift(gram, trans):
    return mm(trans, mm(gram, trans), "tn")


def pack(a):
    return jnp.concatenate([a[: RANK // 2], a[RANK // 2 :]], axis=1)


def unpack(a):
    return jnp.concatenate([a[:, :RANK], a[:, RANK:]], axis=0)


def eliminate(m, pairs, first, last):
    lane = lax.broadcasted_iota(jnp.int32, (1, 1, 128), 2) & (RANK - 1)
    for base in range(first, last, 8):
        rows = RANK - base
        sub = lax.broadcasted_iota(jnp.int32, (1, rows, 1), 1) + base
        half = lax.broadcasted_iota(jnp.int32, (pairs * rows, 128), 1) & RANK

        def step(k, carry, base=base, rows=rows, sub=sub, half=half):
            here = lane == k
            row = m[0:pairs, pl.ds(k, 1), :]
            tail = m[0:pairs, base:RANK, :]
            column = jnp.take_along_axis(
                tail.reshape(pairs * rows, 128), half + k, axis=1, mode="promise_in_bounds"
            ).reshape(pairs, rows, 128)
            pivot = jnp.take_along_axis(
                jnp.broadcast_to(row, (pairs, 8, 128)).reshape(pairs * 8, 128),
                half[: pairs * 8] + k,
                axis=1,
                mode="promise_in_bounds",
            ).reshape(pairs, 8, 128)[:, :1]
            scale = lax.rsqrt(pivot)
            scaled = jnp.where(here, 1.0, row) * scale
            fresh = jnp.where(here, 0.0, tail) - column * (scaled * scale)
            m[0:pairs, base:RANK, :] = jnp.where(
                sub > k, fresh, jnp.where(sub == k, scaled, tail)
            )
            return carry

        lax.fori_loop(base, base + 8, step, 0)


def triangles(a):
    row = lax.broadcasted_iota(jnp.int32, (RANK, RANK), 0)
    col = lax.broadcasted_iota(jnp.int32, (RANK, RANK), 1)
    upper = jnp.where(col > row, a, jnp.where(col == row, 1.0 / a, 0.0))
    inverse = jnp.where(col <= row, a, 0.0)
    return upper, inverse


def tree_kernel(
    row_bits, x_bits,
    basis, transfer, device_transfer, upper_transfer,
    leaf_out, path_out, low_out, edge_out,
    state, path, edge, nodes, total,
    row_buf, z_buf, x_buf, lows, mine,
    edge_sem, row_send, row_recv, z_send, z_recv, x_send, x_recv,
    zl_send, zl_recv, xl_send, xl_recv,
):
    n_rows, n_z, n_x = 2**row_bits, 2**Z_BITS, 2**x_bits
    levels = row_bits + Z_BITS + x_bits
    branch = lax.axis_index("leaf")
    row_id = lax.axis_index("rows")
    x_id = branch // n_z
    z_id = branch % n_z
    leaves = basis.shape[0]
    pairs = leaves // 2

    def to_row(d):
        return {"rows": (row_id + d) % n_rows}

    def to_z(d):
        return {"leaf": x_id * n_z + (z_id + d) % n_z}

    def to_x(d):
        return {"leaf": ((x_id + d) % n_x) * n_z + z_id}

    barrier = pltpu.get_barrier_semaphore()
    for place, count in ((to_row, n_rows), (to_z, n_z), (to_x, n_x)):
        for d in range(1, count):
            pl.semaphore_signal(
                barrier, inc=1, device_id=place(d), device_id_type=pl.DeviceIdType.MESH
            )

    spans = []
    at = 0
    start = branch * n_rows
    count = n_rows
    level = levels
    for bits, begin in ((row_bits, branch), (Z_BITS, x_id), (x_bits, 0)):
        for step in range(bits):
            level -= 1
            count = 2 ** (bits - 1 - step)
            spans.append((at, count, level, 2**level - 2 + begin * count))
            at += count
    fetches = []
    for index, (at, count, level, source) in enumerate(spans):
        if level > 0:
            fetch = pltpu.make_async_copy(
                upper_transfer.at[pl.ds(source, count)],
                nodes.at[pl.ds(at, count)],
                edge_sem.at[index],
            )
            fetch.start()
            fetches.append(fetch)

    total[...] = jnp.zeros_like(total)

    def leaf_pair(p, carry):
        part = None
        grams = []
        for h in range(2):
            b = basis[2 * p + h]
            gram = mm(b, b, "nt")
            trans = transfer[2 * p + h]
            moved = mm(trans, mm(gram, trans), "tn")
            part = moved if part is None else part + moved
            grams.append(gram)
        state[p] = jnp.concatenate(grams, axis=1)
        total[...] += part
        return carry

    lax.fori_loop(0, pairs, leaf_pair, 0)
    own = total[...]
    state[pairs] = jnp.concatenate([own, own], axis=1)
    edge[0] = device_transfer[0]
    row_buf[row_id] = pack(lift(own, device_transfer[0]))
    pl.semaphore_wait(barrier, n_rows - 1 + n_z - 1 + n_x - 1)

    def sends(buf, slot, place, count, send, recv):
        out = []
        for d in range(1, count):
            copy = pltpu.make_async_remote_copy(
                src_ref=buf.at[slot],
                dst_ref=buf.at[slot],
                send_sem=send.at[d - 1],
                recv_sem=recv.at[d - 1],
                device_id=place(d),
                device_id_type=pl.DeviceIdType.MESH,
            )
            copy.start()
            out.append(copy)
        return out

    def receive(buf, slot, place, count, send, recv):
        for d in range(1, count):
            pltpu.make_async_remote_copy(
                src_ref=buf.at[slot],
                dst_ref=buf.at[(slot + count - d) % count],
                send_sem=send.at[d - 1],
                recv_sem=recv.at[d - 1],
                device_id=place(d),
                device_id_type=pl.DeviceIdType.MESH,
            ).wait_recv()

    def climb(buf, bits, which, first):
        lifted = [unpack(buf[i]) for i in range(2**bits)]
        for step in range(bits):
            at, count, level, _ = spans[first + step]
            grams = [lifted[2 * i] + lifted[2 * i + 1] for i in range(count)]
            for i in range(count):
                total_at = path_slots.at[i]
                total_at[...] = grams[i]
            path_rows.append(None)
            chosen = path_slots[which >> (step + 1)]
            slot = first + step
            if slot % 2 == 0:
                path[slot // 2, :, :RANK] = chosen
            else:
                path[slot // 2, :, RANK:] = chosen
            if level > 0:
                fetches[first + step].wait()
                edge[first + step + 1] = nodes[at + (which >> (step + 1))]
                lifted = [lift(grams[i], nodes[at + i]) for i in range(count)]
        return lifted[0]

    path_slots = mine.at[pl.ds(0, 4)]
    path_rows = []

    out = sends(row_buf, row_id, to_row, n_rows, row_send, row_recv)
    eliminate(state, pairs + 1, 0, 8)
    receive(row_buf, row_id, to_row, n_rows, row_send, row_recv)
    z_buf[z_id] = pack(climb(row_buf, row_bits, row_id, 0))
    out += sends(z_buf, z_id, to_z, n_z, z_send, z_recv)
    eliminate(state, pairs + 1, 8, 40)
    receive(z_buf, z_id, to_z, n_z, z_send, z_recv)
    x_buf[x_id] = pack(climb(z_buf, Z_BITS, z_id, row_bits))
    out += sends(x_buf, x_id, to_x, n_x, x_send, x_recv)
    eliminate(state, pairs + 1, 40, RANK)
    own_upper, _ = triangles(state[pairs][:, :RANK])
    lows[x_id, z_id] = pack(own_upper)

    for d in range(1, n_z):
        copy = pltpu.make_async_remote_copy(
            src_ref=lows.at[x_id, z_id],
            dst_ref=lows.at[x_id, z_id],
            send_sem=zl_send.at[d - 1],
            recv_sem=zl_recv.at[d - 1],
            device_id=to_z(d),
            device_id_type=pl.DeviceIdType.MESH,
        )
        copy.start()
        out.append(copy)
    receive(x_buf, x_id, to_x, n_x, x_send, x_recv)
    climb(x_buf, x_bits, x_id, row_bits + Z_BITS)
    for d in range(1, n_z):
        pltpu.make_async_remote_copy(
            src_ref=lows.at[x_id, z_id],
            dst_ref=lows.at[x_id, (z_id + n_z - d) % n_z],
            send_sem=zl_send.at[d - 1],
            recv_sem=zl_recv.at[d - 1],
            device_id=to_z(d),
            device_id_type=pl.DeviceIdType.MESH,
        ).wait_recv()
    out += sends(lows, x_id, to_x, n_x, xl_send, xl_recv)
    eliminate(path, levels // 2, 0, RANK)
    for p in range(pairs + 1):
        leaf_out[p] = state[p]
    path_out[...] = path[...]
    edge_out[...] = edge[...]
    receive(lows, x_id, to_x, n_x, xl_send, xl_recv)
    for x in range(n_x):
        for z in range(n_z):
            low_out[x * n_z + z] = lows[x, z]
    for copy in out:
        copy.wait_send()


def finish_kernel(
    row_bits, levels, step_leaves,
    offsets, basis, transfer, couplings, leaf_state, own_state, path, edge, lows,
    orth_out, bridge_out, trans_out, coupled_out,
    own_upper, own_inverse,
):
    step = pl.program_id(0)
    n_leaf = lows.shape[0]
    branch = lax.axis_index("leaf")

    @pl.when(step == 0)
    def _():
        upper, inverse = triangles(own_state[0][:, :RANK])
        own_upper[...] = upper
        own_inverse[...] = inverse
        for k in range(levels):
            h = (k % 2) * RANK
            above, above_inverse = triangles(path[k // 2][:, h : h + RANK])
            trans_out[0, k] = mm(mm(upper, edge[k]), above_inverse, "nt")
            upper = above

    for i in range(step_leaves):
        h = (i % 2) * RANK
        upper, inverse = triangles(leaf_state[i // 2][:, h : h + RANK])
        orth_out[i] = mm(inverse, basis[i])
        bridge_out[i] = mm(mm(upper, transfer[i]), own_inverse[...], "nt")
        offset = offsets[step * step_leaves + i]
        column = (branch + offset // (2**row_bits)) % n_leaf
        low = unpack(lows[column])
        coupled_out[i] = mm(own_upper[...], mm(couplings[i], low, "nt"))


def per_device(
    leaf_basis, leaf_transfer, device_transfer, upper_transfer, couplings, couple_offset
):
    n_rows = lax.axis_size("rows")
    n_leaf = lax.axis_size("leaf")
    row_bits = n_rows.bit_length() - 1
    x_bits = n_leaf.bit_length() - 1 - Z_BITS
    n_z, n_x = 2**Z_BITS, 2**x_bits
    levels = row_bits + Z_BITS + x_bits
    leaves, _, width = leaf_basis.shape
    pairs = leaves // 2
    f32 = jnp.float32
    vmem = pl.BlockSpec(memory_space=pltpu.VMEM)
    n_nodes = n_rows - 1 + n_z - 1 + n_x - 1
    dma = pltpu.SemaphoreType.DMA
    half = RANK // 2
    leaf_state, path, lows, edge = pl.pallas_call(
        functools.partial(tree_kernel, row_bits, x_bits),
        out_shape=(
            jax.ShapeDtypeStruct((pairs + 1, RANK, 128), f32),
            jax.ShapeDtypeStruct((levels // 2, RANK, 128), f32),
            jax.ShapeDtypeStruct((n_leaf, half, 128), f32),
            jax.ShapeDtypeStruct((levels, RANK, RANK), f32),
        ),
        in_specs=[vmem, vmem, vmem, pl.BlockSpec(memory_space=pl.ANY)],
        out_specs=(vmem, vmem, vmem, vmem),
        scratch_shapes=[
            pltpu.VMEM((pairs + 1, RANK, 128), f32),
            pltpu.VMEM((levels // 2, RANK, 128), f32),
            pltpu.VMEM((levels, RANK, RANK), f32),
            pltpu.VMEM((n_nodes, RANK, RANK), f32),
            pltpu.VMEM((RANK, RANK), f32),
            pltpu.VMEM((n_rows, half, 128), f32),
            pltpu.VMEM((n_z, half, 128), f32),
            pltpu.VMEM((n_x, half, 128), f32),
            pltpu.VMEM((n_x, n_z, half, 128), f32),
            pltpu.VMEM((4, RANK, RANK), f32),
            dma((levels,)),
            dma((n_rows - 1,)), dma((n_rows - 1,)),
            dma((n_z - 1,)), dma((n_z - 1,)),
            dma((n_x - 1,)), dma((n_x - 1,)),
            dma((n_z - 1,)), dma((n_z - 1,)),
            dma((n_x - 1,)), dma((n_x - 1,)),
        ],
        compiler_params=pltpu.CompilerParams(
            collective_id=0, has_side_effects=True, vmem_limit_bytes=40 * 2**20
        ),
    )(leaf_basis, leaf_transfer, device_transfer, upper_transfer)

    chunk = 8
    full = lambda *shape: pl.BlockSpec(shape, lambda i: (0,) * len(shape))
    part = lambda *shape: pl.BlockSpec(shape, lambda i: (i,) + (0,) * (len(shape) - 1))
    return pl.pallas_call(
        functools.partial(finish_kernel, row_bits, levels, chunk),
        grid=(leaves // chunk,),
        out_shape=(
            jax.ShapeDtypeStruct((leaves, RANK, width), f32),
            jax.ShapeDtypeStruct((leaves, RANK, RANK), f32),
            jax.ShapeDtypeStruct((1, levels, RANK, RANK), f32),
            jax.ShapeDtypeStruct((leaves, RANK, RANK), f32),
        ),
        in_specs=[
            pl.BlockSpec(memory_space=pltpu.SMEM),
            part(chunk, RANK, width),
            part(chunk, RANK, RANK),
            part(chunk, RANK, RANK),
            part(chunk // 2, RANK, 128),
            pl.BlockSpec((1, RANK, 128), lambda i: (pairs, 0, 0)),
            full(levels // 2, RANK, 128),
            full(levels, RANK, RANK),
            full(n_leaf, half, 128),
        ],
        out_specs=(
            part(chunk, RANK, width),
            part(chunk, RANK, RANK),
            full(1, levels, RANK, RANK),
            part(chunk, RANK, RANK),
        ),
        scratch_shapes=[pltpu.VMEM((RANK, RANK), f32), pltpu.VMEM((RANK, RANK), f32)],
        compiler_params=pltpu.CompilerParams(vmem_limit_bytes=40 * 2**20),
    )(couple_offset, leaf_basis, leaf_transfer, couplings, leaf_state, leaf_state, path, edge, lows)


def solution(mesh):
    split = P(("leaf", "rows"))
    return jax.shard_map(
        per_device,
        mesh=mesh,
        in_specs=(split, split, split, P(), split, split),
        out_specs=(split, split, split, split),
        check_vma=False,
    )
```

```python
import functools

import jax
import jax.numpy as jnp
from jax import lax
from jax.experimental import pallas as pl
from jax.experimental.pallas import tpu as pltpu
from jax.sharding import PartitionSpec as P

HIGH = lax.Precision.HIGHEST
RANK = 64
HALF = 32
SLOTS = 128
NODES = 256
Z_BITS = 3


def mm(a, b, dims="nn"):
    contract = ((1 if dims[0] == "n" else 0,), (0 if dims[1] == "n" else 1,))
    return lax.dot_general(
        a, b, (contract, ((), ())), precision=HIGH, preferred_element_type=jnp.float32
    )


def lift(grams, trans):
    inner = [mm(g, t) for g, t in zip(grams, trans)]
    return [mm(t, i, "tn") for t, i in zip(trans, inner)]


def pack(a):
    return jnp.concatenate([a[:HALF], a[HALF:]], axis=1)


def unpack(a):
    return jnp.concatenate([a[:, :RANK], a[:, RANK:]], axis=0)


def slot(index):
    return pl.ds(index, HALF, stride=SLOTS)


def eliminate(x):
    sub = lax.broadcasted_iota(jnp.int32, (8, SLOTS), 0)
    group = 4
    for v in range(RANK // 8):
        base = 8 * v
        block = [x[base + t, base : base + 8, :] for t in range(8)]
        scales = []
        for t in range(8):
            scale = lax.rsqrt(jnp.broadcast_to(block[t][t : t + 1], (8, SLOTS)))
            row = jnp.where(sub == t, 1.0, block[t]) * scale
            x[base + t, base : base + 8, :] = row
            scales.append(scale[:1])
            for u in range(t + 1, 8):
                block[u] = jnp.where(sub == t, 0.0, block[u]) - row[u : u + 1] * row
        for lo, hi in ((0, base), (base + 8, RANK)):
            if lo == hi:
                continue
            rows = [x[base + t, lo:hi, :] for t in range(8)]
            for t in range(8):
                row = rows[t] * scales[t]
                x[base + t, lo:hi, :] = row
                for u in range(t + 1, 8):
                    rows[u] = rows[u] - x[base + t, base + u : base + u + 1, :] * row
        if base + 8 == RANK:
            break
        mid = [jnp.where(sub <= t, x[base + t, base : base + 8, :], 0.0) for t in range(8)]
        for later in range(v + 1, RANK // 8):

            def below(g, carry, base=base, later=later, mid=mid):
                first = 8 * later + g * group
                factor = [
                    [x[base + t, pl.ds(first + r, 1), :] for t in range(8)] for r in range(group)
                ]
                for lo, hi in ((0, base), (8 * later, RANK)):
                    for c in range(lo, hi, 8):
                        acc = [x[first + r, c : c + 8, :] for r in range(group)]
                        for t in range(8):
                            row = x[base + t, c : c + 8, :]
                            for r in range(group):
                                acc[r] = acc[r] - factor[r][t] * row
                        for r in range(group):
                            x[first + r, c : c + 8, :] = acc[r]
                for r in range(group):
                    acc = -(factor[r][0] * mid[0])
                    for t in range(1, 8):
                        acc = acc - factor[r][t] * mid[t]
                    x[first + r, base : base + 8, :] = acc
                return carry

            lax.fori_loop(0, 8 // group, below, 0)


def triangles(a):
    lane = lax.broadcasted_iota(jnp.int32, (HALF, 128), 1)
    row = lax.broadcasted_iota(jnp.int32, (HALF, 128), 0) + (lane // RANK) * HALF
    off = (lane & (RANK - 1)) - row
    parts = [a[8 * v : 8 * v + 8] for v in range(HALF // 8)]
    offs = [off[8 * v : 8 * v + 8] for v in range(HALF // 8)]
    diagonal = jnp.ones_like(parts[0])
    for part, o in zip(parts, offs):
        diagonal = jnp.where(o == 0, part, diagonal)
    diagonal = 1.0 / diagonal
    upper = [
        jnp.where(o > 0, part, jnp.where(o == 0, diagonal, 0.0)) for part, o in zip(parts, offs)
    ]
    inverse = [jnp.where(o <= 0, part, 0.0) for part, o in zip(parts, offs)]
    return jnp.concatenate(upper, axis=0), jnp.concatenate(inverse, axis=0)


def tree_kernel(
    row_bits, x_bits,
    basis_in, transfer_in, device_transfer, upper_in,
    factors_out, edge_out,
    basis, transfer, upper, nodes, total, grams, lanes, work,
    row_buf, z_buf, x_buf, cols,
    in_sem, row_send, row_recv, z_send, z_recv, x_send, x_recv,
    zl_send, zl_recv, xl_send, xl_recv,
):
    n_rows, n_z, n_x = 2**row_bits, 2**Z_BITS, 2**x_bits
    levels = row_bits + Z_BITS + x_bits
    branch = lax.axis_index("leaf")
    row_id = lax.axis_index("rows")
    x_id = branch // n_z
    z_id = branch % n_z
    leaves = basis.shape[0]
    columns = leaves
    paths = columns + n_x * n_z

    def to_row(d):
        return {"rows": (row_id + d) % n_rows}

    def to_z(d):
        return {"leaf": x_id * n_z + (z_id + d) % n_z}

    def to_x(d):
        return {"leaf": ((x_id + d) % n_x) * n_z + z_id}

    chunks = 4
    size = leaves // chunks
    fetch_transfer = pltpu.make_async_copy(transfer_in, transfer, in_sem.at[chunks])
    fetches = [
        pltpu.make_async_copy(
            basis_in.at[pl.ds(c * size, size)], basis.at[pl.ds(c * size, size)], in_sem.at[c]
        )
        for c in range(chunks)
    ]
    fetch_upper = pltpu.make_async_copy(upper_in, upper, in_sem.at[chunks + 1])
    fetches[0].start()
    fetch_transfer.start()
    for fetch in fetches[1:]:
        fetch.start()
    fetch_upper.start()

    barrier = pltpu.get_barrier_semaphore()
    for place, count in ((to_row, n_rows), (to_z, n_z), (to_x, n_x)):
        for d in range(1, count):
            pl.semaphore_signal(
                barrier, inc=1, device_id=place(d), device_id_type=pl.DeviceIdType.MESH
            )

    total[...] = jnp.zeros_like(total)

    batch = 8

    def leaf_group(g, carry):
        first = batch * g
        group = [mm(basis[first + h], basis[first + h], "nt") for h in range(batch)]
        moved = [mm(group[h], transfer[first + h]) for h in range(batch)]
        for h in range(batch):
            grams[slot(first + h), :] = pack(group[h])
        trans = transfer[pl.ds(first, batch)].reshape(batch * RANK, RANK)
        total[...] += mm(trans, jnp.concatenate(moved, axis=0), "tn")
        return carry

    fetch_transfer.wait()
    for c in range(chunks):
        fetches[c].wait()
        lax.fori_loop(c * size // batch, (c + 1) * size // batch, leaf_group, 0)
    own = total[...]
    edge_out[0] = pack(device_transfer[0])
    row_buf[row_id] = pack(lift([own], [device_transfer[0]])[0])
    pl.semaphore_wait(barrier, n_rows - 1 + n_z - 1 + n_x - 1)

    def sends(buf, at, place, count, send, recv):
        out = []
        for d in range(1, count):
            copy = pltpu.make_async_remote_copy(
                src_ref=buf.at[at],
                dst_ref=buf.at[at],
                send_sem=send.at[d - 1],
                recv_sem=recv.at[d - 1],
                device_id=place(d),
                device_id_type=pl.DeviceIdType.MESH,
            )
            copy.start()
            out.append(copy)
        return out

    def receive(buf, at, place, count, send, recv):
        for d in range(1, count):
            pltpu.make_async_remote_copy(
                src_ref=buf.at[at],
                dst_ref=buf.at[(at + count - d) % count],
                send_sem=send.at[d - 1],
                recv_sem=recv.at[d - 1],
                device_id=place(d),
                device_id_type=pl.DeviceIdType.MESH,
            ).wait_recv()

    def climb(buf, bits, which, level):
        lifted = [unpack(buf[i]) for i in range(2**bits)]
        for step in range(bits):
            level -= 1
            count = 2 ** (bits - 1 - step)
            own_node = which >> (step + 1)
            rise = [lifted[2 * i] + lifted[2 * i + 1] for i in range(count)]
            for i in range(count):
                work[i] = pack(rise[i])
            k = levels - 1 - level
            grams[slot(paths + k), :] = work[own_node]
            if level > 0:
                start = 2**level - 2 + ((row_id + n_rows * branch) >> (levels - level)) - own_node
                for i in range(count):
                    work[i] = nodes[pl.ds(start + i, HALF, stride=NODES), :]
                edge_out[k + 1] = work[own_node]
                lifted = lift(rise, [unpack(work[i]) for i in range(count)])
        return lifted[0]

    out = sends(row_buf, row_id, to_row, n_rows, row_send, row_recv)
    cols[x_id, z_id] = pack(own)
    for d in range(1, n_z):
        copy = pltpu.make_async_remote_copy(
            src_ref=cols.at[x_id, z_id],
            dst_ref=cols.at[x_id, z_id],
            send_sem=zl_send.at[d - 1],
            recv_sem=zl_recv.at[d - 1],
            device_id=to_z(d),
            device_id_type=pl.DeviceIdType.MESH,
        )
        copy.start()
        out.append(copy)

    fetch_upper.wait()

    def turn(r, carry):
        for lo, hi in ((0, 128), (128, upper.shape[2])):
            both = jnp.concatenate([upper[r, :, lo:hi], upper[HALF + r, :, lo:hi]], axis=0)
            nodes[pl.ds(r * NODES + lo, hi - lo), :] = both.T
        return carry

    lax.fori_loop(0, HALF, turn, 0, unroll=2)
    receive(row_buf, row_id, to_row, n_rows, row_send, row_recv)
    z_buf[z_id] = pack(climb(row_buf, row_bits, row_id, levels))
    out += sends(z_buf, z_id, to_z, n_z, z_send, z_recv)
    for d in range(1, n_z):
        pltpu.make_async_remote_copy(
            src_ref=cols.at[x_id, z_id],
            dst_ref=cols.at[x_id, (z_id + n_z - d) % n_z],
            send_sem=zl_send.at[d - 1],
            recv_sem=zl_recv.at[d - 1],
            device_id=to_z(d),
            device_id_type=pl.DeviceIdType.MESH,
        ).wait_recv()
    out += sends(cols, x_id, to_x, n_x, xl_send, xl_recv)
    receive(z_buf, z_id, to_z, n_z, z_send, z_recv)
    x_buf[x_id] = pack(climb(z_buf, Z_BITS, z_id, levels - row_bits))
    out += sends(x_buf, x_id, to_x, n_x, x_send, x_recv)
    receive(x_buf, x_id, to_x, n_x, x_send, x_recv)
    climb(x_buf, x_bits, x_id, x_bits)
    receive(cols, x_id, to_x, n_x, xl_send, xl_recv)
    for x in range(n_x):
        for z in range(n_z):
            grams[slot(columns + x * n_z + z), :] = cols[x, z]

    def to_lanes(r, carry):
        both = grams[pl.ds(pl.multiple_of(r * SLOTS, SLOTS), SLOTS), :].T
        lanes[r] = both[:RANK]
        lanes[HALF + r] = both[RANK:]
        return carry

    def from_lanes(r, carry):
        both = jnp.concatenate([lanes[r], lanes[HALF + r]], axis=0)
        factors_out[pl.ds(pl.multiple_of(r * SLOTS, SLOTS), SLOTS), :] = both.T
        return carry

    lax.fori_loop(0, HALF, to_lanes, 0, unroll=2)
    eliminate(lanes)
    lax.fori_loop(0, HALF, from_lanes, 0, unroll=2)
    for copy in out:
        copy.wait_send()


def finish_kernel(
    row_bits, levels, step_leaves, leaves, n_leaf,
    offsets, basis, transfer, couplings, factors, edge,
    orth_out, bridge_out, trans_out, coupled_out,
    own_upper, own_inverse,
):
    step = pl.program_id(0)
    branch = lax.axis_index("leaf")

    def factor(index):
        upper, inverse = triangles(factors[slot(index), :])
        return unpack(upper), unpack(inverse)

    @pl.when(step == 0)
    def _():
        upper, inverse = factor(leaves + branch)
        own_upper[...] = upper
        own_inverse[...] = inverse
        above = [factor(leaves + n_leaf + k) for k in range(levels)]
        uppers = [upper] + [a[0] for a in above]
        inner = [mm(uppers[k], unpack(edge[k])) for k in range(levels)]
        for k in range(levels):
            trans_out[0, k] = mm(inner[k], above[k][1], "nt")

    each = range(step_leaves)
    pairs = [factor(step * step_leaves + i) for i in each]
    for i in each:
        orth_out[i] = mm(pairs[i][1], basis[i])
    inner = [mm(pairs[i][0], transfer[i]) for i in each]
    lows = []
    for i in each:
        offset = offsets[step * step_leaves + i]
        column = (branch + offset // (2**row_bits)) % n_leaf
        lows.append(factor(leaves + column)[0])
    right = [mm(couplings[i], lows[i], "nt") for i in each]
    inverse = own_inverse[...]
    upper = own_upper[...]
    for i in each:
        bridge_out[i] = mm(inner[i], inverse, "nt")
    for i in each:
        coupled_out[i] = mm(upper, right[i])


def per_device(
    leaf_basis, leaf_transfer, device_transfer, upper_transfer, couplings, couple_offset
):
    n_rows = lax.axis_size("rows")
    n_leaf = lax.axis_size("leaf")
    row_bits = n_rows.bit_length() - 1
    x_bits = n_leaf.bit_length() - 1 - Z_BITS
    n_z, n_x = 2**Z_BITS, 2**x_bits
    levels = row_bits + Z_BITS + x_bits
    leaves, _, width = leaf_basis.shape
    f32 = jnp.float32
    vmem = pl.BlockSpec(memory_space=pltpu.VMEM)
    hbm = pl.BlockSpec(memory_space=pltpu.HBM)
    dma = pltpu.SemaphoreType.DMA
    upper = jnp.transpose(upper_transfer, (1, 2, 0))
    factors, edge = pl.pallas_call(
        functools.partial(tree_kernel, row_bits, x_bits),
        out_shape=(
            jax.ShapeDtypeStruct((HALF * SLOTS, 128), f32),
            jax.ShapeDtypeStruct((levels, HALF, 128), f32),
        ),
        in_specs=[hbm, hbm, vmem, hbm],
        out_specs=(vmem, vmem),
        scratch_shapes=[
            pltpu.VMEM(leaf_basis.shape, f32),
            pltpu.VMEM(leaf_transfer.shape, f32),
            pltpu.VMEM(upper.shape, f32),
            pltpu.VMEM((HALF * NODES, 128), f32),
            pltpu.VMEM((RANK, RANK), f32),
            pltpu.VMEM((HALF * SLOTS, 128), f32),
            pltpu.VMEM((RANK, RANK, SLOTS), f32),
            pltpu.VMEM((4, HALF, 128), f32),
            pltpu.VMEM((n_rows, HALF, 128), f32),
            pltpu.VMEM((n_z, HALF, 128), f32),
            pltpu.VMEM((n_x, HALF, 128), f32),
            pltpu.VMEM((n_x, n_z, HALF, 128), f32),
            dma((6,)),
            dma((n_rows - 1,)), dma((n_rows - 1,)),
            dma((n_z - 1,)), dma((n_z - 1,)),
            dma((n_x - 1,)), dma((n_x - 1,)),
            dma((n_z - 1,)), dma((n_z - 1,)),
            dma((n_x - 1,)), dma((n_x - 1,)),
        ],
        compiler_params=pltpu.CompilerParams(
            collective_id=0, has_side_effects=True, vmem_limit_bytes=60 * 2**20
        ),
    )(leaf_basis, leaf_transfer, device_transfer, upper)

    chunk = 8
    full = lambda *shape: pl.BlockSpec(shape, lambda i: (0,) * len(shape))
    part = lambda *shape: pl.BlockSpec(shape, lambda i: (i,) + (0,) * (len(shape) - 1))
    return pl.pallas_call(
        functools.partial(finish_kernel, row_bits, levels, chunk, leaves, n_leaf),
        grid=(leaves // chunk,),
        out_shape=(
            jax.ShapeDtypeStruct((leaves, RANK, width), f32),
            jax.ShapeDtypeStruct((leaves, RANK, RANK), f32),
            jax.ShapeDtypeStruct((1, levels, RANK, RANK), f32),
            jax.ShapeDtypeStruct((leaves, RANK, RANK), f32),
        ),
        in_specs=[
            pl.BlockSpec(memory_space=pltpu.SMEM),
            part(chunk, RANK, width),
            part(chunk, RANK, RANK),
            part(chunk, RANK, RANK),
            vmem,
            vmem,
        ],
        out_specs=(
            part(chunk, RANK, width),
            part(chunk, RANK, RANK),
            full(1, levels, RANK, RANK),
            part(chunk, RANK, RANK),
        ),
        scratch_shapes=[pltpu.VMEM((RANK, RANK), f32), pltpu.VMEM((RANK, RANK), f32)],
        compiler_params=pltpu.CompilerParams(vmem_limit_bytes=60 * 2**20),
    )(couple_offset, leaf_basis, leaf_transfer, couplings, factors, edge)


def solution(mesh):
    split = P(("leaf", "rows"))
    return jax.shard_map(
        per_device,
        mesh=mesh,
        in_specs=(split, split, split, P(), split, split),
        out_specs=(split, split, split, split),
        check_vma=False,
    )
```

```python
import functools

import jax
import jax.numpy as jnp
from jax import lax
from jax.experimental import pallas as pl
from jax.experimental.pallas import tpu as pltpu
from jax.sharding import PartitionSpec as P

RANK = 64
HALF = 32
LANES = 128
SLOTS = 72
NODES = 256
Z_BITS = 3


def mm(a, b, dims="nn", precision=lax.Precision.HIGHEST):
    contract = ((1 if dims[0] == "n" else 0,), (0 if dims[1] == "n" else 1,))
    return lax.dot_general(
        a, b, (contract, ((), ())), precision=precision, preferred_element_type=jnp.float32
    )


def split(a):
    high = a.astype(jnp.bfloat16)
    return high, (a - high.astype(jnp.float32)).astype(jnp.bfloat16)


def mm3(a, b, dims="nn"):
    (ah, al), (bh, bl) = (x if isinstance(x, tuple) else split(x) for x in (a, b))
    one = lambda p, q: mm(p, q, dims, lax.Precision.DEFAULT)
    return one(ah, bh) + (one(ah, bl) + one(al, bh))


def lift(grams, trans):
    inner = [mm(g, t) for g, t in zip(grams, trans)]
    return [mm(t, i, "tn") for t, i in zip(trans, inner)]


def pack(a):
    return jnp.concatenate([a[:HALF], a[HALF:]], axis=1)


def unpack(a):
    return jnp.concatenate([a[:, :RANK], a[:, RANK:]], axis=0)


def slot(index):
    return pl.ds(index, HALF, stride=SLOTS)


def eliminate(x):
    sub = lax.broadcasted_iota(jnp.int32, (8, LANES), 0)
    group = 8
    for v in range(RANK // 8):
        base = 8 * v
        block = [x[base + t, base : base + 8, :] for t in range(8)]
        scales = []
        for t in range(8):
            scale = lax.rsqrt(jnp.broadcast_to(block[t][t : t + 1], (8, LANES)))
            row = jnp.where(sub == t, 1.0, block[t]) * scale
            x[base + t, base : base + 8, :] = row
            scales.append(scale[:1])
            for u in range(t + 1, 8):
                block[u] = jnp.where(sub == t, 0.0, block[u]) - row[u : u + 1] * row
        for lo, hi in ((0, base), (base + 8, RANK)):
            if lo == hi:
                continue
            rows = [x[base + t, lo:hi, :] for t in range(8)]
            for t in range(8):
                row = rows[t] * scales[t]
                x[base + t, lo:hi, :] = row
                for u in range(t + 1, 8):
                    rows[u] = rows[u] - x[base + t, base + u : base + u + 1, :] * row
        if base + 8 == RANK:
            break
        mid = [jnp.where(sub <= t, x[base + t, base : base + 8, :], 0.0) for t in range(8)]
        for later in range(v + 1, RANK // 8):

            def below(g, carry, base=base, later=later, mid=mid):
                first = 8 * later + g * group
                factor = [
                    [x[base + t, pl.ds(first + r, 1), :] for t in range(8)] for r in range(group)
                ]
                for lo, hi in ((0, base), (8 * later, RANK)):
                    for c in range(lo, hi, 8):
                        acc = [x[first + r, c : c + 8, :] for r in range(group)]
                        for t in range(8):
                            row = x[base + t, c : c + 8, :]
                            for r in range(group):
                                acc[r] = acc[r] - factor[r][t] * row
                        for r in range(group):
                            x[first + r, c : c + 8, :] = acc[r]
                for r in range(group):
                    acc = -(factor[r][0] * mid[0])
                    for t in range(1, 8):
                        acc = acc - factor[r][t] * mid[t]
                    x[first + r, base : base + 8, :] = acc
                return carry

            lax.fori_loop(0, 8 // group, below, 0)


def triangles(a):
    lane = lax.broadcasted_iota(jnp.int32, (HALF, 128), 1)
    row = lax.broadcasted_iota(jnp.int32, (HALF, 128), 0) + (lane // RANK) * HALF
    off = (lane & (RANK - 1)) - row
    parts = [a[8 * v : 8 * v + 8] for v in range(HALF // 8)]
    offs = [off[8 * v : 8 * v + 8] for v in range(HALF // 8)]
    diagonal = jnp.ones_like(parts[0])
    for part, o in zip(parts, offs):
        diagonal = jnp.where(o == 0, part, diagonal)
    diagonal = 1.0 / diagonal
    upper = [
        jnp.where(o > 0, part, jnp.where(o == 0, diagonal, 0.0)) for part, o in zip(parts, offs)
    ]
    inverse = [jnp.where(o <= 0, part, 0.0) for part, o in zip(parts, offs)]
    return jnp.concatenate(upper, axis=0), jnp.concatenate(inverse, axis=0)


def tree_kernel(
    row_bits, x_bits,
    basis_in, transfer_in, device_transfer, upper_in,
    factors_out, edge_out,
    basis, transfer, upper, nodes, grams, lanes, work,
    row_buf, z_buf, x_buf, cols,
    in_sem, out_sem, row_send, row_recv, z_send, z_recv, x_send, x_recv,
    zl_send, zl_recv, xl_send, xl_recv,
):
    n_rows, n_z, n_x = 2**row_bits, 2**Z_BITS, 2**x_bits
    levels = row_bits + Z_BITS + x_bits
    branch = lax.axis_index("leaf")
    row_id = lax.axis_index("rows")
    x_id = branch // n_z
    z_id = branch % n_z
    leaves = basis.shape[0]
    columns = leaves
    paths = columns + n_x * n_z

    def to_row(d):
        return {"rows": (row_id + d) % n_rows}

    def to_z(d):
        return {"leaf": x_id * n_z + (z_id + d) % n_z}

    def to_x(d):
        return {"leaf": ((x_id + d) % n_x) * n_z + z_id}

    starts = (0, leaves // 4, leaves // 2, leaves)
    chunks = len(starts) - 1
    fetch_transfer = pltpu.make_async_copy(transfer_in, transfer, in_sem.at[chunks])
    fetches = [
        pltpu.make_async_copy(
            basis_in.at[starts[c] : starts[c + 1]], basis.at[starts[c] : starts[c + 1]], in_sem.at[c]
        )
        for c in range(chunks)
    ]
    fetch_upper = pltpu.make_async_copy(upper_in, upper, in_sem.at[chunks + 1])
    fetches[0].start()
    fetch_transfer.start()
    for fetch in fetches[1:]:
        fetch.start()

    barrier = pltpu.get_barrier_semaphore()
    for place, count in ((to_row, n_rows), (to_z, n_z), (to_x, n_x)):
        for d in range(1, count):
            pl.semaphore_signal(
                barrier, inc=1, device_id=place(d), device_id_type=pl.DeviceIdType.MESH
            )


    def leaf_group(first, batch):
        group = [mm(basis[first + h], basis[first + h], "nt") for h in range(batch)]
        if first == 0:
            fetch_transfer.wait()
            fetch_upper.start()
        moved = [mm(group[h], transfer[first + h]) for h in range(batch)]
        for h in range(batch):
            grams[slot(first + h), :] = pack(group[h])
        trans = transfer[first : first + batch].reshape(batch * RANK, RANK)
        return mm(trans, jnp.concatenate(moved, axis=0), "tn")

    own = None
    for c in range(chunks):
        fetches[c].wait()
        part = leaf_group(starts[c], starts[c + 1] - starts[c])
        own = part if own is None else own + part
    edge_out[0] = pack(device_transfer[0])
    row_buf[row_id] = pack(lift([own], [device_transfer[0]])[0])
    pl.semaphore_wait(barrier, n_rows - 1 + n_z - 1 + n_x - 1)

    def sends(buf, at, place, count, send, recv):
        out = []
        for d in sorted(range(1, count), key=lambda d: -min(d, count - d)):
            copy = pltpu.make_async_remote_copy(
                src_ref=buf.at[at],
                dst_ref=buf.at[at],
                send_sem=send.at[d - 1],
                recv_sem=recv.at[d - 1],
                device_id=place(d),
                device_id_type=pl.DeviceIdType.MESH,
            )
            copy.start()
            out.append(copy)
        return out

    def receive(buf, at, place, count, send, recv):
        for d in range(1, count):
            pltpu.make_async_remote_copy(
                src_ref=buf.at[at],
                dst_ref=buf.at[(at + count - d) % count],
                send_sem=send.at[d - 1],
                recv_sem=recv.at[d - 1],
                device_id=place(d),
                device_id_type=pl.DeviceIdType.MESH,
            ).wait_recv()

    def climb(buf, bits, which, level):
        lifted = None
        for step in range(bits):
            level -= 1
            count = 2 ** (bits - 1 - step)
            own_node = which >> (step + 1)
            if step == 0:
                packed = [buf[2 * i] + buf[2 * i + 1] for i in range(count)]
                rise = [unpack(p) for p in packed]
            else:
                rise = [lifted[2 * i] + lifted[2 * i + 1] for i in range(count)]
                packed = [pack(r) for r in rise]
            for i in range(count):
                work[i] = packed[i]
            k = levels - 1 - level
            grams[slot(paths + k), :] = work[own_node]
            if level > 0:
                start = 2**level - 2 + ((row_id + n_rows * branch) >> (levels - level)) - own_node
                for i in range(count):
                    work[i] = nodes[pl.ds(start + i, HALF, stride=NODES), :]
                edge_out[k + 1] = work[own_node]
                lifted = lift(rise, [unpack(work[i]) for i in range(count)])
        return lifted[0]

    out = sends(row_buf, row_id, to_row, n_rows, row_send, row_recv)
    cols[x_id, z_id] = pack(own)
    for d in range(1, n_z):
        copy = pltpu.make_async_remote_copy(
            src_ref=cols.at[x_id, z_id],
            dst_ref=cols.at[x_id, z_id],
            send_sem=zl_send.at[d - 1],
            recv_sem=zl_recv.at[d - 1],
            device_id=to_z(d),
            device_id_type=pl.DeviceIdType.MESH,
        )
        copy.start()
        out.append(copy)

    fetch_upper.wait()

    def turn(r, carry):
        for lo, hi in ((0, 128), (128, upper.shape[2])):
            both = jnp.concatenate([upper[r, :, lo:hi], upper[HALF + r, :, lo:hi]], axis=0)
            nodes[pl.ds(r * NODES + lo, hi - lo), :] = both.T
        return carry

    lax.fori_loop(0, HALF, turn, 0, unroll=4)
    receive(row_buf, row_id, to_row, n_rows, row_send, row_recv)
    z_buf[z_id] = pack(climb(row_buf, row_bits, row_id, levels))
    out += sends(z_buf, z_id, to_z, n_z, z_send, z_recv)
    for d in range(1, n_z):
        pltpu.make_async_remote_copy(
            src_ref=cols.at[x_id, z_id],
            dst_ref=cols.at[x_id, (z_id + n_z - d) % n_z],
            send_sem=zl_send.at[d - 1],
            recv_sem=zl_recv.at[d - 1],
            device_id=to_z(d),
            device_id_type=pl.DeviceIdType.MESH,
        ).wait_recv()
    out += sends(cols, x_id, to_x, n_x, xl_send, xl_recv)
    receive(z_buf, z_id, to_z, n_z, z_send, z_recv)
    x_buf[x_id] = pack(climb(z_buf, Z_BITS, z_id, levels - row_bits))
    out += sends(x_buf, x_id, to_x, n_x, x_send, x_recv)
    receive(x_buf, x_id, to_x, n_x, x_send, x_recv)
    climb(x_buf, x_bits, x_id, x_bits)
    receive(cols, x_id, to_x, n_x, xl_send, xl_recv)
    for x in range(n_x):
        for z in range(n_z):
            grams[slot(columns + x * n_z + z), :] = cols[x, z]

    def rows_of(r):
        return pl.ds(pl.multiple_of(r * SLOTS, 8), SLOTS)

    def to_lanes(r, carry):
        both = grams[rows_of(r), :].T
        lanes[r, :, :SLOTS] = both[:RANK]
        lanes[HALF + r, :, :SLOTS] = both[RANK:]
        return carry

    def from_lanes(r, carry):
        both = jnp.concatenate([lanes[r, :, :SLOTS], lanes[HALF + r, :, :SLOTS]], axis=0)
        grams[rows_of(r), :] = both.T
        return carry

    lax.fori_loop(0, HALF, to_lanes, 0, unroll=4)
    eliminate(lanes)
    parts = 4
    leave = []
    for part in range(parts):
        size = HALF // parts
        lax.fori_loop(part * size, (part + 1) * size, from_lanes, 0, unroll=4)
        span = pl.ds(part * size * SLOTS, size * SLOTS)
        copy = pltpu.make_async_copy(grams.at[span], factors_out.at[span], out_sem.at[part])
        copy.start()
        leave.append(copy)
    for copy in leave:
        copy.wait()
    for copy in out:
        copy.wait_send()


def finish_kernel(
    row_bits, levels, step_leaves, leaves, n_leaf,
    offsets, basis, transfer, couplings, factors, edge,
    orth_out, bridge_out, trans_out, coupled_out,
    own_upper, own_inverse,
):
    step = pl.program_id(0)
    branch = lax.axis_index("leaf")

    def factor(index):
        upper, inverse = triangles(factors[slot(index), :])
        return unpack(upper), unpack(inverse)

    @pl.when(step == 0)
    def _():
        upper, inverse = factor(leaves + branch)
        own_upper[...] = upper
        own_inverse[...] = inverse
        above = [factor(leaves + n_leaf + k) for k in range(levels)]
        uppers = [upper] + [a[0] for a in above]
        inner = [mm3(uppers[k], unpack(edge[k]), "nn") for k in range(levels)]
        for k in range(levels):
            trans_out[0, k] = mm3(inner[k], above[k][1], "nt")

    each = range(step_leaves)
    pairs = [factor(step * step_leaves + i) for i in each]
    for i in each:
        orth_out[i] = mm3(pairs[i][1], basis[i], "nn")
    inner = [mm3(pairs[i][0], transfer[i], "nn") for i in each]
    lows = []
    for i in each:
        offset = offsets[step * step_leaves + i]
        column = (branch + offset // (2**row_bits)) % n_leaf
        lows.append(factor(leaves + column)[0])
    right = [mm3(couplings[i], lows[i], "nt") for i in each]
    inverse = split(own_inverse[...])
    upper = split(own_upper[...])
    for i in each:
        bridge_out[i] = mm3(inner[i], inverse, "nt")
    for i in each:
        coupled_out[i] = mm3(upper, right[i], "nn")


def per_device(
    leaf_basis, leaf_transfer, device_transfer, upper_transfer, couplings, couple_offset
):
    n_rows = lax.axis_size("rows")
    n_leaf = lax.axis_size("leaf")
    row_bits = n_rows.bit_length() - 1
    x_bits = n_leaf.bit_length() - 1 - Z_BITS
    n_z, n_x = 2**Z_BITS, 2**x_bits
    levels = row_bits + Z_BITS + x_bits
    leaves, _, width = leaf_basis.shape
    f32 = jnp.float32
    vmem = pl.BlockSpec(memory_space=pltpu.VMEM)
    hbm = pl.BlockSpec(memory_space=pltpu.HBM)
    dma = pltpu.SemaphoreType.DMA
    upper = jnp.transpose(upper_transfer, (1, 2, 0))
    factors, edge = pl.pallas_call(
        functools.partial(tree_kernel, row_bits, x_bits),
        out_shape=(
            jax.ShapeDtypeStruct((HALF * SLOTS, 128), f32),
            jax.ShapeDtypeStruct((levels, HALF, 128), f32),
        ),
        in_specs=[hbm, hbm, vmem, hbm],
        out_specs=(hbm, vmem),
        scratch_shapes=[
            pltpu.VMEM(leaf_basis.shape, f32),
            pltpu.VMEM(leaf_transfer.shape, f32),
            pltpu.VMEM(upper.shape, f32),
            pltpu.VMEM((HALF * NODES, 128), f32),
            pltpu.VMEM((HALF * SLOTS, 128), f32),
            pltpu.VMEM((RANK, RANK, LANES), f32),
            pltpu.VMEM((4, HALF, 128), f32),
            pltpu.VMEM((n_rows, HALF, 128), f32),
            pltpu.VMEM((n_z, HALF, 128), f32),
            pltpu.VMEM((n_x, HALF, 128), f32),
            pltpu.VMEM((n_x, n_z, HALF, 128), f32),
            dma((5,)), dma((4,)),
            dma((n_rows - 1,)), dma((n_rows - 1,)),
            dma((n_z - 1,)), dma((n_z - 1,)),
            dma((n_x - 1,)), dma((n_x - 1,)),
            dma((n_z - 1,)), dma((n_z - 1,)),
            dma((n_x - 1,)), dma((n_x - 1,)),
        ],
        compiler_params=pltpu.CompilerParams(
            collective_id=0, has_side_effects=True, vmem_limit_bytes=60 * 2**20
        ),
    )(leaf_basis, leaf_transfer, device_transfer, upper)

    chunk = 8
    full = lambda *shape: pl.BlockSpec(shape, lambda i: (0,) * len(shape))
    part = lambda *shape: pl.BlockSpec(shape, lambda i: (i,) + (0,) * (len(shape) - 1))
    return pl.pallas_call(
        functools.partial(finish_kernel, row_bits, levels, chunk, leaves, n_leaf),
        grid=(leaves // chunk,),
        out_shape=(
            jax.ShapeDtypeStruct((leaves, RANK, width), f32),
            jax.ShapeDtypeStruct((leaves, RANK, RANK), f32),
            jax.ShapeDtypeStruct((1, levels, RANK, RANK), f32),
            jax.ShapeDtypeStruct((leaves, RANK, RANK), f32),
        ),
        in_specs=[
            pl.BlockSpec(memory_space=pltpu.SMEM),
            part(chunk, RANK, width),
            part(chunk, RANK, RANK),
            part(chunk, RANK, RANK),
            vmem,
            vmem,
        ],
        out_specs=(
            part(chunk, RANK, width),
            part(chunk, RANK, RANK),
            full(1, levels, RANK, RANK),
            part(chunk, RANK, RANK),
        ),
        scratch_shapes=[pltpu.VMEM((RANK, RANK), f32), pltpu.VMEM((RANK, RANK), f32)],
        compiler_params=pltpu.CompilerParams(vmem_limit_bytes=60 * 2**20),
    )(couple_offset, leaf_basis, leaf_transfer, couplings, factors, edge)


def solution(mesh):
    split = P(("leaf", "rows"))
    return jax.shard_map(
        per_device,
        mesh=mesh,
        in_specs=(split, split, split, P(), split, split),
        out_specs=(split, split, split, split),
        check_vma=False,
    )
```

```python
import functools

import jax
import jax.numpy as jnp
from jax import lax
from jax.experimental import pallas as pl
from jax.experimental.pallas import tpu as pltpu
from jax.sharding import PartitionSpec as P

RANK = 64
HALF = 32
LANES = 128
SLOTS = 72
NODES = 256
Z_BITS = 3


def mm(a, b, dims="nn", precision=lax.Precision.HIGHEST):
    contract = ((1 if dims[0] == "n" else 0,), (0 if dims[1] == "n" else 1,))
    return lax.dot_general(
        a, b, (contract, ((), ())), precision=precision, preferred_element_type=jnp.float32
    )


def split(a):
    high = a.astype(jnp.bfloat16)
    return high, (a - high.astype(jnp.float32)).astype(jnp.bfloat16)


def mm3(a, b, dims="nn"):
    (ah, al), (bh, bl) = (x if isinstance(x, tuple) else split(x) for x in (a, b))
    one = lambda p, q: mm(p, q, dims, lax.Precision.DEFAULT)
    return one(ah, bh) + (one(ah, bl) + one(al, bh))


def lift(grams, trans):
    inner = [mm(g, t) for g, t in zip(grams, trans)]
    return [mm(t, i, "tn") for t, i in zip(trans, inner)]


def pack(a):
    return jnp.concatenate([a[:HALF], a[HALF:]], axis=1)


def unpack(a):
    return jnp.concatenate([a[:, :RANK], a[:, RANK:]], axis=0)


def slot(index):
    return pl.ds(index, HALF, stride=SLOTS)


def eliminate(x):
    sub = lax.broadcasted_iota(jnp.int32, (8, LANES), 0)
    group = 8
    for v in range(RANK // 8):
        base = 8 * v
        block = [x[base + t, base : base + 8, :] for t in range(8)]
        scales = []
        for t in range(8):
            scale = lax.rsqrt(jnp.broadcast_to(block[t][t : t + 1], (8, LANES)))
            row = jnp.where(sub == t, 1.0, block[t]) * scale
            x[base + t, base : base + 8, :] = row
            scales.append(scale[:1])
            for u in range(t + 1, 8):
                block[u] = jnp.where(sub == t, 0.0, block[u]) - row[u : u + 1] * row
        for lo, hi in ((0, base), (base + 8, RANK)):
            if lo == hi:
                continue
            rows = [x[base + t, lo:hi, :] for t in range(8)]
            for t in range(8):
                row = rows[t] * scales[t]
                x[base + t, lo:hi, :] = row
                for u in range(t + 1, 8):
                    rows[u] = rows[u] - x[base + t, base + u : base + u + 1, :] * row
        if base + 8 == RANK:
            break
        mid = [jnp.where(sub <= t, x[base + t, base : base + 8, :], 0.0) for t in range(8)]
        for later in range(v + 1, RANK // 8):

            def below(g, carry, base=base, later=later, mid=mid):
                first = 8 * later + g * group
                factor = [
                    [x[base + t, pl.ds(first + r, 1), :] for t in range(8)] for r in range(group)
                ]
                for lo, hi in ((0, base), (8 * later, RANK)):
                    for c in range(lo, hi, 8):
                        acc = [x[first + r, c : c + 8, :] for r in range(group)]
                        for t in range(8):
                            row = x[base + t, c : c + 8, :]
                            for r in range(group):
                                acc[r] = acc[r] - factor[r][t] * row
                        for r in range(group):
                            x[first + r, c : c + 8, :] = acc[r]
                for r in range(group):
                    acc = -(factor[r][0] * mid[0])
                    for t in range(1, 8):
                        acc = acc - factor[r][t] * mid[t]
                    x[first + r, base : base + 8, :] = acc
                return carry

            lax.fori_loop(0, 8 // group, below, 0)


def triangles(a):
    lane = lax.broadcasted_iota(jnp.int32, (HALF, 128), 1)
    row = lax.broadcasted_iota(jnp.int32, (HALF, 128), 0) + (lane // RANK) * HALF
    off = (lane & (RANK - 1)) - row
    parts = [a[8 * v : 8 * v + 8] for v in range(HALF // 8)]
    offs = [off[8 * v : 8 * v + 8] for v in range(HALF // 8)]
    diagonal = jnp.ones_like(parts[0])
    for part, o in zip(parts, offs):
        diagonal = jnp.where(o == 0, part, diagonal)
    diagonal = 1.0 / diagonal
    upper = [
        jnp.where(o > 0, part, jnp.where(o == 0, diagonal, 0.0)) for part, o in zip(parts, offs)
    ]
    inverse = [jnp.where(o <= 0, part, 0.0) for part, o in zip(parts, offs)]
    return jnp.concatenate(upper, axis=0), jnp.concatenate(inverse, axis=0)


def tree_kernel(
    row_bits, x_bits,
    basis_in, transfer_in, device_transfer, upper_in,
    factors_out, edge_out,
    basis, transfer, upper, nodes, grams, lanes, work,
    row_buf, z_buf, x_buf, cols,
    in_sem, out_sem, row_send, row_recv, z_send, z_recv, x_send, x_recv,
    zl_send, zl_recv, xl_send, xl_recv,
):
    n_rows, n_z, n_x = 2**row_bits, 2**Z_BITS, 2**x_bits
    levels = row_bits + Z_BITS + x_bits
    branch = lax.axis_index("leaf")
    row_id = lax.axis_index("rows")
    x_id = branch // n_z
    z_id = branch % n_z
    leaves = basis.shape[0]
    columns = leaves
    paths = columns + n_x * n_z

    def to_row(d):
        return {"rows": (row_id + d) % n_rows}

    def to_z(d):
        return {"leaf": x_id * n_z + (z_id + d) % n_z}

    def to_x(d):
        return {"leaf": ((x_id + d) % n_x) * n_z + z_id}

    starts = (0, leaves // 4, leaves // 2, leaves)
    chunks = len(starts) - 1
    fetch_transfer = pltpu.make_async_copy(transfer_in, transfer, in_sem.at[chunks])
    fetches = [
        pltpu.make_async_copy(
            basis_in.at[starts[c] : starts[c + 1]], basis.at[starts[c] : starts[c + 1]], in_sem.at[c]
        )
        for c in range(chunks)
    ]
    quarter = RANK // 4
    fetch_upper = [
        pltpu.make_async_copy(
            upper_in.at[pl.ds(q * quarter, quarter)],
            upper.at[pl.ds(q * quarter, quarter)],
            in_sem.at[chunks + 1 + q],
        )
        for q in range(4)
    ]
    fetches[0].start()
    fetch_transfer.start()
    fetches[1].start()
    for fetch in fetch_upper:
        fetch.start()
    fetches[2].start()

    barrier = pltpu.get_barrier_semaphore()
    for place, count in ((to_row, n_rows), (to_z, n_z), (to_x, n_x)):
        for d in range(1, count):
            pl.semaphore_signal(
                barrier, inc=1, device_id=place(d), device_id_type=pl.DeviceIdType.MESH
            )


    def leaf_group(first, batch):
        group = [mm(basis[first + h], basis[first + h], "nt") for h in range(batch)]
        if first == 0:
            fetch_transfer.wait()
        moved = [mm(group[h], transfer[first + h]) for h in range(batch)]
        for h in range(batch):
            grams[slot(first + h), :] = pack(group[h])
        trans = transfer[first : first + batch].reshape(batch * RANK, RANK)
        return mm(trans, jnp.concatenate(moved, axis=0), "tn")

    def turn(r):
        for lo, hi in ((0, 128), (128, upper.shape[2])):
            both = jnp.concatenate([upper[r, :, lo:hi], upper[HALF + r, :, lo:hi]], axis=0)
            nodes[r * NODES + lo : r * NODES + hi, :] = both.T

    own = None
    for c in range(chunks):
        fetches[c].wait()
        if c == chunks - 1:
            for fetch in fetch_upper:
                fetch.wait()
            for r in range(HALF):
                turn(r)
        part = leaf_group(starts[c], starts[c + 1] - starts[c])
        own = part if own is None else own + part
    edge_out[0] = pack(device_transfer[0])
    row_buf[row_id] = pack(lift([own], [device_transfer[0]])[0])
    pl.semaphore_wait(barrier, n_rows - 1 + n_z - 1 + n_x - 1)

    def sends(buf, at, place, count, send, recv):
        out = []
        for d in sorted(range(1, count), key=lambda d: -min(d, count - d)):
            copy = pltpu.make_async_remote_copy(
                src_ref=buf.at[at],
                dst_ref=buf.at[at],
                send_sem=send.at[d - 1],
                recv_sem=recv.at[d - 1],
                device_id=place(d),
                device_id_type=pl.DeviceIdType.MESH,
            )
            copy.start()
            out.append(copy)
        return out

    def receive(buf, at, place, count, send, recv):
        for d in range(1, count):
            pltpu.make_async_remote_copy(
                src_ref=buf.at[at],
                dst_ref=buf.at[(at + count - d) % count],
                send_sem=send.at[d - 1],
                recv_sem=recv.at[d - 1],
                device_id=place(d),
                device_id_type=pl.DeviceIdType.MESH,
            ).wait_recv()

    def climb(buf, bits, which, level):
        lifted = None
        for step in range(bits):
            level -= 1
            count = 2 ** (bits - 1 - step)
            own_node = which >> (step + 1)
            if step == 0:
                packed = [buf[2 * i] + buf[2 * i + 1] for i in range(count)]
                rise = [unpack(p) for p in packed]
            else:
                rise = [lifted[2 * i] + lifted[2 * i + 1] for i in range(count)]
                packed = [pack(r) for r in rise]
            for i in range(count):
                work[i] = packed[i]
            k = levels - 1 - level
            grams[slot(paths + k), :] = work[own_node]
            if level > 0:
                start = 2**level - 2 + ((row_id + n_rows * branch) >> (levels - level)) - own_node
                for i in range(count):
                    work[i] = nodes[pl.ds(start + i, HALF, stride=NODES), :]
                edge_out[k + 1] = work[own_node]
                lifted = lift(rise, [unpack(work[i]) for i in range(count)])
        return lifted[0]

    out = sends(row_buf, row_id, to_row, n_rows, row_send, row_recv)
    cols[x_id, z_id] = pack(own)
    for d in range(1, n_z):
        copy = pltpu.make_async_remote_copy(
            src_ref=cols.at[x_id, z_id],
            dst_ref=cols.at[x_id, z_id],
            send_sem=zl_send.at[d - 1],
            recv_sem=zl_recv.at[d - 1],
            device_id=to_z(d),
            device_id_type=pl.DeviceIdType.MESH,
        )
        copy.start()
        out.append(copy)

    receive(row_buf, row_id, to_row, n_rows, row_send, row_recv)
    z_buf[z_id] = pack(climb(row_buf, row_bits, row_id, levels))
    out += sends(z_buf, z_id, to_z, n_z, z_send, z_recv)
    for d in range(1, n_z):
        pltpu.make_async_remote_copy(
            src_ref=cols.at[x_id, z_id],
            dst_ref=cols.at[x_id, (z_id + n_z - d) % n_z],
            send_sem=zl_send.at[d - 1],
            recv_sem=zl_recv.at[d - 1],
            device_id=to_z(d),
            device_id_type=pl.DeviceIdType.MESH,
        ).wait_recv()
    out += sends(cols, x_id, to_x, n_x, xl_send, xl_recv)
    receive(z_buf, z_id, to_z, n_z, z_send, z_recv)
    x_buf[x_id] = pack(climb(z_buf, Z_BITS, z_id, levels - row_bits))
    out += sends(x_buf, x_id, to_x, n_x, x_send, x_recv)
    receive(x_buf, x_id, to_x, n_x, x_send, x_recv)
    climb(x_buf, x_bits, x_id, x_bits)
    receive(cols, x_id, to_x, n_x, xl_send, xl_recv)
    for x in range(n_x):
        for z in range(n_z):
            grams[slot(columns + x * n_z + z), :] = cols[x, z]

    def rows_of(r):
        return pl.ds(pl.multiple_of(r * SLOTS, 8), SLOTS)

    def to_lanes(r, carry):
        both = grams[rows_of(r), :].T
        lanes[r, :, :SLOTS] = both[:RANK]
        lanes[HALF + r, :, :SLOTS] = both[RANK:]
        return carry

    def from_lanes(r, carry):
        both = jnp.concatenate([lanes[r, :, :SLOTS], lanes[HALF + r, :, :SLOTS]], axis=0)
        grams[rows_of(r), :] = both.T
        return carry

    lax.fori_loop(0, HALF, to_lanes, 0, unroll=8)
    eliminate(lanes)
    parts = 4
    leave = []
    for part in range(parts):
        size = HALF // parts
        lax.fori_loop(part * size, (part + 1) * size, from_lanes, 0, unroll=8)
        span = pl.ds(part * size * SLOTS, size * SLOTS)
        copy = pltpu.make_async_copy(grams.at[span], factors_out.at[span], out_sem.at[part])
        copy.start()
        leave.append(copy)
    for copy in out:
        copy.wait_send()
    for copy in leave:
        copy.wait()


def finish_kernel(
    row_bits, levels, step_leaves, leaves, n_leaf,
    offsets, basis, transfer, couplings, factors, edge,
    orth_out, bridge_out, trans_out, coupled_out,
    own_upper, own_inverse,
):
    step = pl.program_id(0)
    branch = lax.axis_index("leaf")

    def factor(index):
        upper, inverse = triangles(factors[slot(index), :])
        return unpack(upper), unpack(inverse)

    @pl.when(step == 0)
    def _():
        upper, inverse = factor(leaves + branch)
        own_upper[...] = upper
        own_inverse[...] = inverse
        above = [factor(leaves + n_leaf + k) for k in range(levels)]
        uppers = [upper] + [a[0] for a in above]
        inner = [mm3(uppers[k], unpack(edge[k]), "nn") for k in range(levels)]
        for k in range(levels):
            trans_out[0, k] = mm3(inner[k], above[k][1], "nt")

    each = range(step_leaves)
    pairs = [factor(step * step_leaves + i) for i in each]
    for i in each:
        orth_out[i] = mm3(pairs[i][1], basis[i], "nn")
    inner = [mm3(pairs[i][0], transfer[i], "nn") for i in each]
    lows = []
    for i in each:
        offset = offsets[step * step_leaves + i]
        column = (branch + offset // (2**row_bits)) % n_leaf
        lows.append(factor(leaves + column)[0])
    right = [mm3(couplings[i], lows[i], "nt") for i in each]
    inverse = split(own_inverse[...])
    upper = split(own_upper[...])
    for i in each:
        bridge_out[i] = mm3(inner[i], inverse, "nt")
    for i in each:
        coupled_out[i] = mm3(upper, right[i], "nn")


def per_device(
    leaf_basis, leaf_transfer, device_transfer, upper_transfer, couplings, couple_offset
):
    n_rows = lax.axis_size("rows")
    n_leaf = lax.axis_size("leaf")
    row_bits = n_rows.bit_length() - 1
    x_bits = n_leaf.bit_length() - 1 - Z_BITS
    n_z, n_x = 2**Z_BITS, 2**x_bits
    levels = row_bits + Z_BITS + x_bits
    leaves, _, width = leaf_basis.shape
    f32 = jnp.float32
    vmem = pl.BlockSpec(memory_space=pltpu.VMEM)
    hbm = pl.BlockSpec(memory_space=pltpu.HBM)
    dma = pltpu.SemaphoreType.DMA
    upper = jnp.transpose(upper_transfer, (1, 2, 0))
    factors, edge = pl.pallas_call(
        functools.partial(tree_kernel, row_bits, x_bits),
        out_shape=(
            jax.ShapeDtypeStruct((HALF * SLOTS, 128), f32),
            jax.ShapeDtypeStruct((levels, HALF, 128), f32),
        ),
        in_specs=[hbm, hbm, vmem, hbm],
        out_specs=(hbm, vmem),
        scratch_shapes=[
            pltpu.VMEM(leaf_basis.shape, f32),
            pltpu.VMEM(leaf_transfer.shape, f32),
            pltpu.VMEM(upper.shape, f32),
            pltpu.VMEM((HALF * NODES, 128), f32),
            pltpu.VMEM((HALF * SLOTS, 128), f32),
            pltpu.VMEM((RANK, RANK, LANES), f32),
            pltpu.VMEM((4, HALF, 128), f32),
            pltpu.VMEM((n_rows, HALF, 128), f32),
            pltpu.VMEM((n_z, HALF, 128), f32),
            pltpu.VMEM((n_x, HALF, 128), f32),
            pltpu.VMEM((n_x, n_z, HALF, 128), f32),
            dma((8,)), dma((4,)),
            dma((n_rows - 1,)), dma((n_rows - 1,)),
            dma((n_z - 1,)), dma((n_z - 1,)),
            dma((n_x - 1,)), dma((n_x - 1,)),
            dma((n_z - 1,)), dma((n_z - 1,)),
            dma((n_x - 1,)), dma((n_x - 1,)),
        ],
        compiler_params=pltpu.CompilerParams(
            collective_id=0, has_side_effects=True, vmem_limit_bytes=60 * 2**20
        ),
    )(leaf_basis, leaf_transfer, device_transfer, upper)

    chunk = 8
    full = lambda *shape: pl.BlockSpec(shape, lambda i: (0,) * len(shape))
    part = lambda *shape: pl.BlockSpec(shape, lambda i: (i,) + (0,) * (len(shape) - 1))
    return pl.pallas_call(
        functools.partial(finish_kernel, row_bits, levels, chunk, leaves, n_leaf),
        grid=(leaves // chunk,),
        out_shape=(
            jax.ShapeDtypeStruct((leaves, RANK, width), f32),
            jax.ShapeDtypeStruct((leaves, RANK, RANK), f32),
            jax.ShapeDtypeStruct((1, levels, RANK, RANK), f32),
            jax.ShapeDtypeStruct((leaves, RANK, RANK), f32),
        ),
        in_specs=[
            pl.BlockSpec(memory_space=pltpu.SMEM),
            part(chunk, RANK, width),
            part(chunk, RANK, RANK),
            part(chunk, RANK, RANK),
            vmem,
            vmem,
        ],
        out_specs=(
            part(chunk, RANK, width),
            part(chunk, RANK, RANK),
            full(1, levels, RANK, RANK),
            part(chunk, RANK, RANK),
        ),
        scratch_shapes=[pltpu.VMEM((RANK, RANK), f32), pltpu.VMEM((RANK, RANK), f32)],
        compiler_params=pltpu.CompilerParams(vmem_limit_bytes=60 * 2**20),
    )(couple_offset, leaf_basis, leaf_transfer, couplings, factors, edge)


def solution(mesh):
    split = P(("leaf", "rows"))
    return jax.shard_map(
        per_device,
        mesh=mesh,
        in_specs=(split, split, split, P(), split, split),
        out_specs=(split, split, split, split),
        check_vma=False,
    )
```

```python
import functools

import jax
import jax.numpy as jnp
from jax import lax
from jax.experimental import pallas as pl
from jax.experimental.pallas import tpu as pltpu
from jax.sharding import PartitionSpec as P

RANK = 64
HALF = 32
LANES = 128
SLOTS = 72
NODES = 256
Z_BITS = 3


def mm(a, b, dims="nn", precision=lax.Precision.HIGHEST):
    contract = ((1 if dims[0] == "n" else 0,), (0 if dims[1] == "n" else 1,))
    return lax.dot_general(
        a, b, (contract, ((), ())), precision=precision, preferred_element_type=jnp.float32
    )


def split(a):
    high = a.astype(jnp.bfloat16)
    return high, (a - high.astype(jnp.float32)).astype(jnp.bfloat16)


def mm3(a, b, dims="nn"):
    (ah, al), (bh, bl) = (x if isinstance(x, tuple) else split(x) for x in (a, b))
    one = lambda p, q: mm(p, q, dims, lax.Precision.DEFAULT)
    return one(ah, bh) + (one(ah, bl) + one(al, bh))


def lift(grams, trans):
    inner = [mm(g, t) for g, t in zip(grams, trans)]
    return [mm(t, i, "tn") for t, i in zip(trans, inner)]


def pack(a):
    return jnp.concatenate([a[:HALF], a[HALF:]], axis=1)


def unpack(a):
    return jnp.concatenate([a[:, :RANK], a[:, RANK:]], axis=0)


def slot(index):
    return pl.ds(index, HALF, stride=SLOTS)


def eliminate(x):
    sub = lax.broadcasted_iota(jnp.int32, (8, LANES), 0)
    group = 8
    for v in range(RANK // 8):
        base = 8 * v
        block = [x[base + t, base : base + 8, :] for t in range(8)]
        scales = []
        for t in range(8):
            scale = lax.rsqrt(jnp.broadcast_to(block[t][t : t + 1], (8, LANES)))
            row = jnp.where(sub == t, 1.0, block[t]) * scale
            x[base + t, base : base + 8, :] = row
            scales.append(scale[:1])
            for u in range(t + 1, 8):
                block[u] = jnp.where(sub == t, 0.0, block[u]) - row[u : u + 1] * row
        for lo, hi in ((0, base), (base + 8, RANK)):
            if lo == hi:
                continue
            rows = [x[base + t, lo:hi, :] for t in range(8)]
            for t in range(8):
                row = rows[t] * scales[t]
                x[base + t, lo:hi, :] = row
                for u in range(t + 1, 8):
                    rows[u] = rows[u] - x[base + t, base + u : base + u + 1, :] * row
        if base + 8 == RANK:
            break
        mid = [jnp.where(sub <= t, x[base + t, base : base + 8, :], 0.0) for t in range(8)]
        for later in range(v + 1, RANK // 8):

            def below(g, carry, base=base, later=later, mid=mid):
                first = 8 * later + g * group
                factor = [
                    [x[base + t, pl.ds(first + r, 1), :] for t in range(8)] for r in range(group)
                ]
                for lo, hi in ((0, base), (8 * later, RANK)):
                    for c in range(lo, hi, 8):
                        acc = [x[first + r, c : c + 8, :] for r in range(group)]
                        for t in range(8):
                            row = x[base + t, c : c + 8, :]
                            for r in range(group):
                                acc[r] = acc[r] - factor[r][t] * row
                        for r in range(group):
                            x[first + r, c : c + 8, :] = acc[r]
                for r in range(group):
                    acc = -(factor[r][0] * mid[0])
                    for t in range(1, 8):
                        acc = acc - factor[r][t] * mid[t]
                    x[first + r, base : base + 8, :] = acc
                return carry

            lax.fori_loop(0, 8 // group, below, 0)


def triangles(a):
    lane = lax.broadcasted_iota(jnp.int32, (HALF, 128), 1)
    row = lax.broadcasted_iota(jnp.int32, (HALF, 128), 0) + (lane // RANK) * HALF
    off = (lane & (RANK - 1)) - row
    parts = [a[8 * v : 8 * v + 8] for v in range(HALF // 8)]
    offs = [off[8 * v : 8 * v + 8] for v in range(HALF // 8)]
    diagonal = jnp.ones_like(parts[0])
    for part, o in zip(parts, offs):
        diagonal = jnp.where(o == 0, part, diagonal)
    diagonal = 1.0 / diagonal
    upper = [
        jnp.where(o > 0, part, jnp.where(o == 0, diagonal, 0.0)) for part, o in zip(parts, offs)
    ]
    inverse = [jnp.where(o <= 0, part, 0.0) for part, o in zip(parts, offs)]
    return jnp.concatenate(upper, axis=0), jnp.concatenate(inverse, axis=0)


def tree_kernel(
    row_bits, x_bits,
    basis_in, transfer_in, device_transfer, upper_in,
    factors_out, edge_out,
    basis, transfer, upper, nodes, grams, lanes, work,
    row_buf, z_buf, x_buf, cols,
    in_sem, out_sem, row_send, row_recv, z_send, z_recv, x_send, x_recv,
    zl_send, zl_recv, xl_send, xl_recv,
):
    n_rows, n_z, n_x = 2**row_bits, 2**Z_BITS, 2**x_bits
    levels = row_bits + Z_BITS + x_bits
    branch = lax.axis_index("leaf")
    row_id = lax.axis_index("rows")
    x_id = branch // n_z
    z_id = branch % n_z
    leaves = basis.shape[0]
    columns = leaves
    paths = columns + n_x * n_z

    def to_row(d):
        return {"rows": (row_id + d) % n_rows}

    def to_z(d):
        return {"leaf": x_id * n_z + (z_id + d) % n_z}

    def to_x(d):
        return {"leaf": ((x_id + d) % n_x) * n_z + z_id}

    starts = (0, leaves // 4, leaves // 2, leaves)
    chunks = len(starts) - 1
    fetch_transfer = pltpu.make_async_copy(transfer_in, transfer, in_sem.at[chunks])
    fetches = [
        pltpu.make_async_copy(
            basis_in.at[starts[c] : starts[c + 1]], basis.at[starts[c] : starts[c + 1]], in_sem.at[c]
        )
        for c in range(chunks)
    ]
    quarter = RANK // 4
    fetch_upper = [
        pltpu.make_async_copy(
            upper_in.at[pl.ds(q * quarter, quarter)],
            upper.at[pl.ds(q * quarter, quarter)],
            in_sem.at[chunks + 1 + q],
        )
        for q in range(4)
    ]
    fetches[0].start()
    fetch_transfer.start()
    fetches[1].start()
    for fetch in fetch_upper:
        fetch.start()
    fetches[2].start()

    barrier = pltpu.get_barrier_semaphore()
    for place, count in ((to_row, n_rows), (to_z, n_z), (to_x, n_x)):
        for d in range(1, count):
            pl.semaphore_signal(
                barrier, inc=1, device_id=place(d), device_id_type=pl.DeviceIdType.MESH
            )


    def leaf_group(first, batch):
        group = [mm(basis[first + h], basis[first + h], "nt") for h in range(batch)]
        if first == 0:
            fetch_transfer.wait()
        moved = [mm(group[h], transfer[first + h]) for h in range(batch)]
        for h in range(batch):
            grams[slot(first + h), :] = pack(group[h])
        trans = transfer[first : first + batch].reshape(batch * RANK, RANK)
        return mm(trans, jnp.concatenate(moved, axis=0), "tn")

    def turn(r):
        for lo, hi in ((0, 128), (128, upper.shape[2])):
            both = jnp.concatenate([upper[r, :, lo:hi], upper[HALF + r, :, lo:hi]], axis=0)
            nodes[r * NODES + lo : r * NODES + hi, :] = both.T

    own = None
    for c in range(chunks):
        fetches[c].wait()
        if c == chunks - 1:
            for fetch in fetch_upper:
                fetch.wait()
            for r in range(HALF):
                turn(r)
        part = leaf_group(starts[c], starts[c + 1] - starts[c])
        own = part if own is None else own + part
    edge_out[0] = pack(device_transfer[0])
    row_buf[row_id] = pack(lift([own], [device_transfer[0]])[0])
    pl.semaphore_wait(barrier, n_rows - 1 + n_z - 1 + n_x - 1)

    def sends(buf, at, place, count, send, recv):
        out = []
        for d in sorted(range(1, count), key=lambda d: -min(d, count - d)):
            copy = pltpu.make_async_remote_copy(
                src_ref=buf.at[at],
                dst_ref=buf.at[at],
                send_sem=send.at[d - 1],
                recv_sem=recv.at[d - 1],
                device_id=place(d),
                device_id_type=pl.DeviceIdType.MESH,
            )
            copy.start()
            out.append(copy)
        return out

    def receive(buf, at, place, count, send, recv):
        for d in range(1, count):
            pltpu.make_async_remote_copy(
                src_ref=buf.at[at],
                dst_ref=buf.at[(at + count - d) % count],
                send_sem=send.at[d - 1],
                recv_sem=recv.at[d - 1],
                device_id=place(d),
                device_id_type=pl.DeviceIdType.MESH,
            ).wait_recv()

    def gather(bits, which, level):
        trans = []
        for step in range(bits):
            level -= 1
            if level > 0:
                own = 2**level - 2 + ((row_id + n_rows * branch) >> (levels - level))
                start = own - (which >> (step + 1))
                edge_out[levels - level] = nodes[pl.ds(own, HALF, stride=NODES), :]
                trans.append(
                    [
                        unpack(nodes[pl.ds(start + i, HALF, stride=NODES), :])
                        for i in range(2 ** (bits - 1 - step))
                    ]
                )
        return trans

    def climb(buf, bits, which, level, trans):
        lifted = None
        for step in range(bits):
            level -= 1
            count = 2 ** (bits - 1 - step)
            own_node = which >> (step + 1)
            if step == 0:
                packed = [buf[2 * i] + buf[2 * i + 1] for i in range(count)]
                rise = [unpack(p) for p in packed]
            else:
                rise = [lifted[2 * i] + lifted[2 * i + 1] for i in range(count)]
                packed = [pack(r) for r in rise]
            for i in range(count):
                work[i] = packed[i]
            k = levels - 1 - level
            grams[slot(paths + k), :] = work[own_node]
            if level > 0:
                lifted = lift(rise, trans[step])
        return lifted[0]

    out = sends(row_buf, row_id, to_row, n_rows, row_send, row_recv)
    cols[x_id, z_id] = pack(own)
    for d in range(1, n_z):
        copy = pltpu.make_async_remote_copy(
            src_ref=cols.at[x_id, z_id],
            dst_ref=cols.at[x_id, z_id],
            send_sem=zl_send.at[d - 1],
            recv_sem=zl_recv.at[d - 1],
            device_id=to_z(d),
            device_id_type=pl.DeviceIdType.MESH,
        )
        copy.start()
        out.append(copy)

    trans = gather(row_bits, row_id, levels)
    receive(row_buf, row_id, to_row, n_rows, row_send, row_recv)
    z_buf[z_id] = pack(climb(row_buf, row_bits, row_id, levels, trans))
    out += sends(z_buf, z_id, to_z, n_z, z_send, z_recv)
    for d in range(1, n_z):
        pltpu.make_async_remote_copy(
            src_ref=cols.at[x_id, z_id],
            dst_ref=cols.at[x_id, (z_id + n_z - d) % n_z],
            send_sem=zl_send.at[d - 1],
            recv_sem=zl_recv.at[d - 1],
            device_id=to_z(d),
            device_id_type=pl.DeviceIdType.MESH,
        ).wait_recv()
    out += sends(cols, x_id, to_x, n_x, xl_send, xl_recv)
    trans = gather(Z_BITS, z_id, levels - row_bits)
    receive(z_buf, z_id, to_z, n_z, z_send, z_recv)
    x_buf[x_id] = pack(climb(z_buf, Z_BITS, z_id, levels - row_bits, trans))
    out += sends(x_buf, x_id, to_x, n_x, x_send, x_recv)
    trans = gather(x_bits, x_id, x_bits)
    receive(x_buf, x_id, to_x, n_x, x_send, x_recv)
    climb(x_buf, x_bits, x_id, x_bits, trans)
    receive(cols, x_id, to_x, n_x, xl_send, xl_recv)
    for x in range(n_x):
        for z in range(n_z):
            grams[slot(columns + x * n_z + z), :] = cols[x, z]

    def rows_of(r):
        return pl.ds(pl.multiple_of(r * SLOTS, 8), SLOTS)

    def to_lanes(r, carry):
        both = grams[rows_of(r), :].T
        lanes[r, :, :SLOTS] = both[:RANK]
        lanes[HALF + r, :, :SLOTS] = both[RANK:]
        return carry

    def from_lanes(r, carry):
        both = jnp.concatenate([lanes[r, :, :SLOTS], lanes[HALF + r, :, :SLOTS]], axis=0)
        grams[rows_of(r), :] = both.T
        return carry

    lax.fori_loop(0, HALF, to_lanes, 0, unroll=8)
    eliminate(lanes)
    parts = 4
    leave = []
    for part in range(parts):
        size = HALF // parts
        lax.fori_loop(part * size, (part + 1) * size, from_lanes, 0, unroll=8)
        span = pl.ds(part * size * SLOTS, size * SLOTS)
        copy = pltpu.make_async_copy(grams.at[span], factors_out.at[span], out_sem.at[part])
        copy.start()
        leave.append(copy)
    for copy in out:
        copy.wait_send()
    for copy in leave:
        copy.wait()


def finish_kernel(
    row_bits, levels, step_leaves, leaves, n_leaf,
    offsets, basis, transfer, couplings, factors, edge,
    orth_out, bridge_out, trans_out, coupled_out,
    own_upper, own_inverse,
):
    step = pl.program_id(0)
    branch = lax.axis_index("leaf")

    def factor(index):
        upper, inverse = triangles(factors[slot(index), :])
        return unpack(upper), unpack(inverse)

    @pl.when(step == 0)
    def _():
        upper, inverse = factor(leaves + branch)
        own_upper[...] = upper
        own_inverse[...] = inverse
        above = [factor(leaves + n_leaf + k) for k in range(levels)]
        uppers = [upper] + [a[0] for a in above]
        inner = [mm3(uppers[k], unpack(edge[k]), "nn") for k in range(levels)]
        for k in range(levels):
            trans_out[0, k] = mm3(inner[k], above[k][1], "nt")

    each = range(step_leaves)
    pairs = [factor(step * step_leaves + i) for i in each]
    for i in each:
        orth_out[i] = mm3(pairs[i][1], basis[i], "nn")
    inner = [mm3(pairs[i][0], transfer[i], "nn") for i in each]
    lows = []
    for i in each:
        offset = offsets[step * step_leaves + i]
        column = (branch + offset // (2**row_bits)) % n_leaf
        lows.append(factor(leaves + column)[0])
    right = [mm3(couplings[i], lows[i], "nt") for i in each]
    inverse = split(own_inverse[...])
    upper = split(own_upper[...])
    for i in each:
        bridge_out[i] = mm3(inner[i], inverse, "nt")
    for i in each:
        coupled_out[i] = mm3(upper, right[i], "nn")


def per_device(
    leaf_basis, leaf_transfer, device_transfer, upper_transfer, couplings, couple_offset
):
    n_rows = lax.axis_size("rows")
    n_leaf = lax.axis_size("leaf")
    row_bits = n_rows.bit_length() - 1
    x_bits = n_leaf.bit_length() - 1 - Z_BITS
    n_z, n_x = 2**Z_BITS, 2**x_bits
    levels = row_bits + Z_BITS + x_bits
    leaves, _, width = leaf_basis.shape
    f32 = jnp.float32
    vmem = pl.BlockSpec(memory_space=pltpu.VMEM)
    hbm = pl.BlockSpec(memory_space=pltpu.HBM)
    dma = pltpu.SemaphoreType.DMA
    upper = jnp.transpose(upper_transfer, (1, 2, 0))
    factors, edge = pl.pallas_call(
        functools.partial(tree_kernel, row_bits, x_bits),
        out_shape=(
            jax.ShapeDtypeStruct((HALF * SLOTS, 128), f32),
            jax.ShapeDtypeStruct((levels, HALF, 128), f32),
        ),
        in_specs=[hbm, hbm, vmem, hbm],
        out_specs=(hbm, vmem),
        scratch_shapes=[
            pltpu.VMEM(leaf_basis.shape, f32),
            pltpu.VMEM(leaf_transfer.shape, f32),
            pltpu.VMEM(upper.shape, f32),
            pltpu.VMEM((HALF * NODES, 128), f32),
            pltpu.VMEM((HALF * SLOTS, 128), f32),
            pltpu.VMEM((RANK, RANK, LANES), f32),
            pltpu.VMEM((4, HALF, 128), f32),
            pltpu.VMEM((n_rows, HALF, 128), f32),
            pltpu.VMEM((n_z, HALF, 128), f32),
            pltpu.VMEM((n_x, HALF, 128), f32),
            pltpu.VMEM((n_x, n_z, HALF, 128), f32),
            dma((8,)), dma((4,)),
            dma((n_rows - 1,)), dma((n_rows - 1,)),
            dma((n_z - 1,)), dma((n_z - 1,)),
            dma((n_x - 1,)), dma((n_x - 1,)),
            dma((n_z - 1,)), dma((n_z - 1,)),
            dma((n_x - 1,)), dma((n_x - 1,)),
        ],
        compiler_params=pltpu.CompilerParams(
            collective_id=0, has_side_effects=True, vmem_limit_bytes=60 * 2**20
        ),
    )(leaf_basis, leaf_transfer, device_transfer, upper)

    chunk = 8
    full = lambda *shape: pl.BlockSpec(shape, lambda i: (0,) * len(shape))
    part = lambda *shape: pl.BlockSpec(shape, lambda i: (i,) + (0,) * (len(shape) - 1))
    return pl.pallas_call(
        functools.partial(finish_kernel, row_bits, levels, chunk, leaves, n_leaf),
        grid=(leaves // chunk,),
        out_shape=(
            jax.ShapeDtypeStruct((leaves, RANK, width), f32),
            jax.ShapeDtypeStruct((leaves, RANK, RANK), f32),
            jax.ShapeDtypeStruct((1, levels, RANK, RANK), f32),
            jax.ShapeDtypeStruct((leaves, RANK, RANK), f32),
        ),
        in_specs=[
            pl.BlockSpec(memory_space=pltpu.SMEM),
            part(chunk, RANK, width),
            part(chunk, RANK, RANK),
            part(chunk, RANK, RANK),
            vmem,
            vmem,
        ],
        out_specs=(
            part(chunk, RANK, width),
            part(chunk, RANK, RANK),
            full(1, levels, RANK, RANK),
            part(chunk, RANK, RANK),
        ),
        scratch_shapes=[pltpu.VMEM((RANK, RANK), f32), pltpu.VMEM((RANK, RANK), f32)],
        compiler_params=pltpu.CompilerParams(vmem_limit_bytes=60 * 2**20),
    )(couple_offset, leaf_basis, leaf_transfer, couplings, factors, edge)


def solution(mesh):
    split = P(("leaf", "rows"))
    return jax.shard_map(
        per_device,
        mesh=mesh,
        in_specs=(split, split, split, P(), split, split),
        out_specs=(split, split, split, split),
        check_vma=False,
    )
```
